768 devices in a mesh: wide: 48 (over x, z), narrow: 16 (over y, core).
Axes of the slice: x: 4, y: 8, z: 12, core: 2. Of those that a mesh axis runs over, the one named last changes fastest.
Arguments:
- agg_rows: bfloat16 [6144, 3840], P('wide'), may hold values from -6 to 6
- seed_feats: bfloat16 [6144, 768], P('wide'), may hold values from -6 to 6
- seed_type: int32 [6144], P('wide'), may hold values from 0 to 1
- w_rel: bfloat16 [3840, 1024], P(None, 'narrow'), may hold values from -0.09375 to 0.09375
- w_self: bfloat16 [2, 768, 1024], P(None, None, 'narrow'), may hold values from -0.21875 to 0.21875
- cotangent: float32 [6144, 1024], P('wide', 'narrow'), may hold values from -6 to 6
- counts: int32 [6144, 5], P('wide'), may hold values from 1 to 25
- owner: int32 [768000, 1], P('wide'), may hold values from 0 to 47; in each aligned block of 1000 rows (0 to 999, 1000 to 1999, ...) at most 26 rows name the same one
- local_row: int32 [768000], P('wide'), may hold values from 0 to 511
Outputs:
- table_grad: float32 [24576, 768], P('wide')
- grad_rel: float32 [3840, 1024], P(None, 'narrow')
- grad_self: float32 [2, 768, 1024], P(None, None, 'narrow')
The draws below stay inside these ranges and needn't reach their ends.
Inputs may be any that keep to these rules, and one draw needn't show every extreme that they name: In each aligned block of 1000 slots no owner appears more than 26 times, and some owner appears exactly 26 times in some block; every owner appears somewhere.
All inputs are finite; a program needn't handle non-finite values.
Results may differ from the reference program's by a relative error of at most 0.0041.
Values may be sent and summed in bfloat16 or wider, within the bound.
A program may use at most 64 MiB of HBM per device.

```python
import math
import jax
import jax.numpy as jnp
import numpy as np
from jax import lax

F = 768
H = 1024
R = 5
FAN = 25
TYPES = 2
NODES_DEV = 512
SEEDS = 6144
NODES = 24576
SLOTS = 768000
BLOCK = 1000
CAP = 26
N_WIDE = 48


def touch_ends(values, own_key, least, high):
    shape = values.shape
    index_at = [jax.random.randint(jax.random.fold_in(own_key, axis), (), 0, shape[axis]) for axis in range(len(shape))]
    values = values.at[tuple(index_at)].set(least)
    longest = shape.index(max(shape))
    index_at[longest] = (index_at[longest] + 1) % shape[longest]
    return values.at[tuple(index_at)].set(high)


def strengthened(result, stream_key, source, target, blocks, factor):
    def block_of(position):
        return (jnp.arange(result.shape[position]) // (result.shape[position] // blocks)).reshape((-1,) + (1,) * (result.ndim - 1 - position))

    one_side = jax.random.permutation(stream_key, blocks)[block_of(target)]
    second = (block_of(target) + blocks // 2) % blocks
    return jnp.where((block_of(source) == one_side) | (block_of(source) == second), factor * result, result)


def steps_of(rng, shape, pieces, least, top_value):
    level, own = 1.0, jax.random.fold_in(rng, 6)
    for dim, shards_of in pieces:
        draws = jnp.exp(jax.random.uniform(jax.random.fold_in(own, dim), (shards_of,), jnp.float32, least / len(pieces), top_value / len(pieces)))
        level = level * jnp.repeat(draws, shape[dim] // shards_of).reshape([-1 if axis == dim else 1 for axis in range(len(shape))])
    return level


def assign_block(stream_key, own, number, rows, amount, top, reach, skew):
    ranking = jax.random.permutation(stream_key, amount)
    packed, common = portions_of(amount, rows * top, reach, skew, True), portions_of(amount, rows * top, reach, skew, False)
    places = jnp.arange(amount)

    def named(tallies, offset_by):
        used = int((tallies > 0).sum())
        fixed = max(1, used // 4)
        passed = fixed + (places - fixed + offset_by * (used - fixed)) % max(1, amount - fixed)
        return jnp.zeros((amount,), jnp.int32).at[ranking[jnp.where(places < fixed, places, passed)]].set(jnp.asarray(tallies, jnp.int32))

    tallies = jnp.where(number % 4 == 0, named(packed, number // 4), named(common, number - number // 4 - 1))
    mixed = jax.random.permutation(jax.random.fold_in(own, 3), amount)
    source_of, taker = mixed[0:amount // 2 * 2:2], mixed[1:amount // 2 * 2:2]
    room = jnp.minimum(tallies[source_of] - 1, reach - tallies[taker]) // 2
    room = jnp.where((source_of == ranking[0]) | (taker == ranking[0]) | (tallies[taker] == 0), 0, jnp.maximum(room, 0))
    passed = jax.random.randint(jax.random.fold_in(own, 4), (amount // 2,), 0, 1 << 20) % (room + 1)
    tallies = tallies.at[source_of].add(-passed).at[taker].add(passed)
    labels = jnp.searchsorted(jnp.cumsum(tallies), jnp.arange(rows * top), side="right").astype(jnp.int32)
    table = labels.reshape(top, rows).T
    table = table[jax.random.permutation(jax.random.fold_in(own, 1), rows)]
    offset_by = jax.random.randint(jax.random.fold_in(own, 2), (rows, 1), 0, top)
    return jnp.take_along_axis(table, (jnp.arange(top)[None, :] + offset_by) % top, axis=1)


def portions_of(number_of, total, most, skew, full):
    loads = [(1 << 20) // math.isqrt(grade ** skew) + 1 for grade in range(1, number_of + 1)]
    largest = most if full else min(most, max(-(-total // number_of), total * loads[0] // sum(loads)))
    least = 1 if total - largest >= number_of - 1 else 0
    given, rest = [largest] + [least] * (number_of - 1), total - largest - least * (number_of - 1)
    while rest > 0:
        candidates = [i for i in range(1, number_of) if given[i] < largest] or [i for i in range(1, number_of) if given[i] < most]
        mass, remaining = sum([loads[i] for i in candidates]), rest
        for i in candidates:
            more = min(most - given[i], max(1, remaining * loads[i] // mass), rest)
            given[i] = given[i] + more
            rest = rest - more
    return np.array(given)


def normal_values(stream_key, shape, scale, reach, split=(), kind=jnp.bfloat16):
    factor_of = steps_of(stream_key, shape, split, -0.22, 0.18) if split else 1.0
    entries = jax.random.normal(stream_key, shape, jnp.float32) * scale * factor_of
    return jnp.minimum(jnp.maximum(entries, -reach), reach).astype(kind)


def gaussian_with(key, shape, scale, reach, cuts, heavy, dtype=jnp.bfloat16):
    array = scale * jax.random.normal(key, shape, jnp.float32)
    if cuts:
        array = array * steps_of(key, shape, cuts, -0.22, 0.18)
    return jnp.clip(strengthened(array, jax.random.fold_in(key, 3), *heavy), -reach, reach).astype(dtype)


def setup_inputs(seed: int = 0) -> dict:
    streams_of = jax.random.split(jax.random.key(seed), 10)
    agg_rows = gaussian_with(streams_of[0], (SEEDS, R * F), 1.0, 6.0, ((0, 48),), (0, 1, 48, 3.25))
    seed_feats = normal_values(streams_of[1], (SEEDS, F), 1.0, 6.0, ((0, 48),))
    seed_type = touch_ends(jax.random.randint(streams_of[2], (SEEDS,), 0, TYPES), jax.random.fold_in(streams_of[2], 1), 0, TYPES - 1).astype(jnp.int32)
    w_rel = normal_values(streams_of[3], (R * F, H), (R * F) ** -0.5, 0.09375, ((1, 16),))
    w_self = normal_values(streams_of[4], (TYPES, F, H), F ** -0.5, 0.21875, ((2, 16),))
    cotangent = normal_values(streams_of[5], (SEEDS, H), 1.0, 6.0, ((0, 48), (1, 16)), jnp.float32)
    counts = touch_ends(jax.random.randint(streams_of[6], (SEEDS, R), 1, FAN + 1), jax.random.fold_in(streams_of[6], 1), 1, FAN).astype(jnp.int32)
    owner_keys = jax.random.split(jax.random.fold_in(streams_of[7], 1), SLOTS // BLOCK)
    owner_turns = jax.random.permutation(jax.random.fold_in(streams_of[7], 3), SLOTS // BLOCK)
    owner = jax.vmap(lambda own, number: assign_block(jax.random.fold_in(streams_of[7], 2), own, number, BLOCK, N_WIDE, 1, CAP, 2))(owner_keys, owner_turns).reshape((SLOTS, 1))
    local_row = touch_ends(jax.random.randint(streams_of[8], (SLOTS,), 0, NODES_DEV), jax.random.fold_in(streams_of[8], 1), 0, NODES_DEV - 1).astype(jnp.int32)
    return {"agg_rows": agg_rows, "seed_feats": seed_feats, "seed_type": seed_type, "w_rel": w_rel, "w_self": w_self, "cotangent": cotangent, "counts": counts, "owner": owner, "local_row": local_row}


def reference(agg_rows, seed_feats, seed_type, w_rel, w_self, cotangent, counts, owner, local_row):
    pre_rel = jnp.dot(agg_rows, w_rel, preferred_element_type=jnp.float32)
    self_zero = jnp.dot(seed_feats, w_self[0], preferred_element_type=jnp.float32)
    self_one = jnp.dot(seed_feats, w_self[1], preferred_element_type=jnp.float32)
    pre = pre_rel + jnp.where(seed_type[:, None] == 0, self_zero, self_one)
    sigma = jax.nn.sigmoid(pre)
    dpre = (cotangent * sigma * (1.0 + pre * (1.0 - sigma))).astype(jnp.bfloat16)
    dims = (((0,), (0,)), ((), ()))
    grad_rel = lax.dot_general(agg_rows, dpre, dims, preferred_element_type=jnp.float32)
    zero_b = jnp.zeros_like(dpre)
    grad_self = jnp.stack([
        lax.dot_general(seed_feats, jnp.where(seed_type[:, None] == t, dpre, zero_b), dims, preferred_element_type=jnp.float32)
        for t in range(TYPES)])
    d_agg = lax.dot_general(dpre, w_rel, (((1,), (1,)), ((), ())), preferred_element_type=jnp.float32)
    d_agg = d_agg.reshape(SEEDS, R, F)
    msg = (d_agg / counts[:, :, None].astype(jnp.float32)).astype(jnp.bfloat16)
    node = (owner[:, 0] * NODES_DEV + local_row).reshape(SEEDS, R, FAN)

    def add_slot(slot, table):
        live = slot < counts
        rows = jnp.where(live[:, :, None], msg, jnp.zeros_like(msg)).astype(jnp.float32)
        names = lax.dynamic_index_in_dim(node, slot, 2, keepdims=False)
        return table.at[names.reshape(-1)].add(rows.reshape(SEEDS * R, F))

    table_grad = lax.fori_loop(0, FAN, add_slot, jnp.zeros((NODES, F), jnp.float32))
    return table_grad, grad_rel, grad_self
```

```python
import functools

import jax
import jax.numpy as jnp
from jax import lax
from jax.experimental import pallas as pl
from jax.experimental.pallas import tpu as pltpu
from jax.sharding import PartitionSpec as P

FAN = 25
NODES_DEV = 512
REL = 5
F = 768
HALF = 384
HID = 64
XN, ZN, YN = 4, 12, 8
GROUP = 16
RA = 3
PA, PB = RA * HALF, (REL - RA) * HALF
GCOLS = REL * F + 2 * F
GWIN = 512
MESH = pl.DeviceIdType.MESH
f32, bf16, i32 = jnp.float32, jnp.bfloat16, jnp.int32


def window_start(k):
    return 128 * ((7 * k) // 2)


def kernel(agg, wr, seeds, ws, kind, cot, cnt, key, tout, gout,
           wother, dp, dother, dsend, dbuf, kall, kf, c_ref, ma, mb,
           wx, wbx, wz, wbz, gz, gx, tsend, tbuf, tall,
           s_w, r_w, s_dp, r_dp, s_kx, r_kx, s_kz, r_kz, s_d, r_d, s_wx, r_wx, s_wz, r_wz,
           s_ax, r_ax, s_az, r_az, s_bx, r_bx, s_bz, r_bz, s_gz, r_gz, s_gx, r_gx,
           s_t, r_t, s_ta, r_ta, s_tc, r_tc):
    wide, narrow = lax.axis_index("wide"), lax.axis_index("narrow")
    x, z = wide // ZN, wide % ZN
    y, core = narrow // 2, narrow % 2
    other = 1 - core

    def at_x(p):
        return (p * ZN + z, narrow)

    def at_z(p):
        return (x * ZN + p, narrow)

    def at_y(p):
        return (wide, p * 2 + core)

    partner = (wide, y * 2 + other)

    def copy(src, dst, s, r, to):
        return pltpu.make_async_remote_copy(
            src_ref=src, dst_ref=dst, send_sem=s, recv_sem=r, device_id=to, device_id_type=MESH)

    barrier = pltpu.get_barrier_semaphore()

    def greet(to):
        pl.semaphore_signal(barrier, inc=1, device_id=to, device_id_type=MESH)

    def each(n, fn):
        def step(d, carry):
            fn(d)
            return carry
        lax.fori_loop(1, n, step, 0)

    each(XN, lambda d: greet(at_x((x + d) % XN)))
    each(ZN, lambda d: greet(at_z((z + d) % ZN)))
    each(YN, lambda d: greet(at_y((y + d) % YN)))
    greet(partner)
    pl.semaphore_wait(barrier, XN + ZN + YN - 2)

    def cp_w(r):
        cols = pl.ds(pl.multiple_of(r * F + other * HALF, 128), HALF)
        return copy(wr.at[:, cols], wother.at[:, pl.ds(r * HALF, HALF)], s_w.at[r], r_w.at[r], partner)

    def cp_kx(d):
        return copy(kall.at[z, x], kall.at[z, x], s_kx.at[d], r_kx.at[d], at_x((x + d) % XN))

    def cp_kz(d):
        return copy(kall.at[z], kall.at[z], s_kz.at[d], r_kz.at[d], at_z((z + d) % ZN))

    def cp_d(d):
        p = (y + d) % YN
        return copy(dsend.at[p], dbuf.at[y], s_d.at[d], r_d.at[d], at_y(p))

    def cp_wx(d):
        p = (x + d) % XN
        return copy(wx.at[p], wbx.at[x], s_wx.at[d], r_wx.at[d], at_x(p))

    def cp_wz(d):
        p = (z + d) % ZN
        return copy(wz.at[p], wbz.at[z], s_wz.at[d], r_wz.at[d], at_z(p))

    def cp_gz(d):
        return copy(gz.at[z], gz.at[z], s_gz.at[d], r_gz.at[d], at_z((z + d) % ZN))

    def cp_gx(d):
        return copy(gz, gx.at[x], s_gx.at[d], r_gx.at[d], at_x((x + d) % XN))

    def cp_t(d):
        p = (y + d) % YN
        return copy(tsend.at[p], tbuf.at[y], s_t.at[d], r_t.at[d], at_y(p))

    def cp_ta(d):
        return copy(tall.at[core, y], tall.at[core, y], s_ta.at[d], r_ta.at[d], at_y((y + d) % YN))

    def cp_tc(d):
        p = (y - d + YN) % YN
        return copy(tall.at[core, p], tall.at[core, p], s_tc.at[d], r_tc.at[d], partner)

    def cp_ax(d):
        return copy(ma.at[z, x], ma.at[z, x], s_ax.at[d], r_ax.at[d], at_x((x + d) % XN))

    def held(direction, t):
        return (z - (t - 1) + ZN) % ZN if direction == 0 else (z + (t - 1)) % ZN

    def next_z(direction):
        return at_z((z + 1) % ZN if direction == 0 else (z + ZN - 1) % ZN)

    def cp_az(direction, t, h):
        part = ma.at[held(direction, t), pl.ds(2 * h, 2)]
        i = (direction * 6 + t - 1) * 2 + h
        return copy(part, part, s_az.at[i], r_az.at[i], next_z(direction))

    def az_parts(t):
        return [(0, 0), (1, 0), (0, 1), (1, 1)] if t < 6 else [(0, 0), (1, 1)]

    def cp_bz(direction, t):
        cols = pl.ds(0, PB) if t < 6 else pl.ds(direction * (PB // 2), PB // 2)
        part = mb.at[held(direction, t), x, :, cols]
        i = direction * 6 + t - 1
        return copy(part, part, s_bz.at[i], r_bz.at[i], next_z(direction))

    def cp_bx(d, piece):
        if piece <= 5:
            p = (z - piece + ZN) % ZN
        elif piece <= 10:
            p = (z + piece - 5) % ZN
        else:
            p = (z + 6) % ZN
        part = mb.at[p, x]
        i = piece * XN + d
        return copy(part, part, s_bx.at[i], r_bx.at[i], at_x((x + d) % XN))

    def start(fn, n):
        each(n, lambda d: fn(d).start())

    def arrive(fn, n):
        each(n, lambda d: fn(d).wait_recv())

    for r in range(REL):
        cp_w(r).start()
    kall[z, x] = key[...]
    start(cp_kx, XN)

    contract = (((1,), (1,)), ((), ()))
    pre = lax.dot_general(wr[...], agg[...], contract, preferred_element_type=f32)
    zero = lax.dot_general(ws[0], seeds[...], contract, preferred_element_type=f32)
    one = lax.dot_general(ws[1], seeds[...], contract, preferred_element_type=f32)
    first = kind[...] == 0
    pre = pre + jnp.where(first, zero, one)
    sigma = 1.0 / (1.0 + jnp.exp(-pre))
    dpre = cot[...] * sigma * (1.0 + pre * (1.0 - sigma))
    dpre_b = dpre.astype(bf16)
    dp[...] = dpre_b
    cp_dp = copy(dp, dother, s_dp, r_dp, partner)
    cp_dp.start()

    for r in range(REL):
        g = jnp.dot(dpre_b, agg[:, r * F:(r + 1) * F], preferred_element_type=f32).astype(bf16)
        for p in range(XN):
            wx[p, :, r * F:(r + 1) * F] = g[p * 16:(p + 1) * 16]
    for t in range(2):
        mask = first if t == 0 else jnp.logical_not(first)
        part = jnp.where(mask, dpre_b.astype(f32), 0.0).astype(bf16)
        g = jnp.dot(part, seeds[...], preferred_element_type=f32).astype(bf16)
        for p in range(XN):
            wx[p, :, (REL + t) * F:(REL + t + 1) * F] = g[p * 16:(p + 1) * 16]

    mine = dpre_b.astype(f32).T.astype(bf16)
    cp_dp.wait_recv()
    theirs = dother[...].astype(f32).T.astype(bf16)
    for r in range(REL):
        cp_w(r).wait_recv()
        cols = pl.ds(pl.multiple_of(r * F + core * HALF, 128), HALF)
        d = jnp.dot(mine, wr[:, cols], preferred_element_type=f32)
        d = d + jnp.dot(theirs, wother[:, r * HALF:(r + 1) * HALF], preferred_element_type=f32)
        d = d.astype(bf16)
        for p in range(YN):
            dsend[p, :, r * HALF:(r + 1) * HALF] = d[p * GROUP:(p + 1) * GROUP]
    start(cp_d, YN)
    start(cp_wx, XN)

    arrive(cp_kx, XN)
    start(cp_kz, ZN)

    arrive(cp_wx, XN)
    for r in range(7):
        cols = slice(r * F, (r + 1) * F)
        total = wx[x, :, cols].astype(f32)
        for d in range(1, XN):
            total = total + wbx[(x + XN - d) % XN, :, cols].astype(f32)
        wx[x, :, cols] = total.astype(bf16)
    for k in range(ZN):
        wz[k] = wx[x, :, window_start(k):window_start(k) + GWIN]
    start(cp_wz, ZN)

    arrive(cp_d, YN)
    for r in range(REL):
        cols = slice(r * HALF, (r + 1) * HALF)
        total = dsend[y, :, cols].astype(f32)
        for d in range(1, YN):
            total = total + dbuf[(y + YN - d) % YN, :, cols].astype(f32)
        message = (total / cnt[:, r:r + 1]).astype(bf16)
        if r < RA:
            ma[z, x, :, cols] = message
        else:
            mb[z, x, :, (r - RA) * HALF:(r - RA + 1) * HALF] = message

    def send_b(t):
        for direction in range(2):
            cp_bz(direction, t).start()

    def take_b(t):
        for direction in range(2):
            cp_bz(direction, t).wait_recv()
        if t < 6:
            send_b(t + 1)
            start(lambda d: cp_bx(d, t), XN)
            start(lambda d: cp_bx(d, 5 + t), XN)
        else:
            start(lambda d: cp_bx(d, 11), XN)

    def send_a(t, part):
        cp_az(part[0], t, part[1]).start()

    def take_a(t):
        for part in az_parts(t):
            cp_az(part[0], t, part[1]).wait_recv()
            if t < 6 and part in az_parts(t + 1):
                send_a(t + 1, part)

    send_b(1)
    start(cp_ax, XN)
    start(lambda d: cp_bx(d, 0), XN)

    arrive(cp_kz, ZN)
    base = (wide * NODES_DEV).astype(f32)
    keys = kall[...].reshape(XN * ZN * GROUP, 128).astype(f32).T
    for hh in range(2):
        v = keys - (base + 256.0 * hh)
        kf[hh] = jnp.where((v >= 0.0) & (v < 256.0), v, -1.0)

    def build(r, part):
        rows = lax.broadcasted_iota(i32, (256, 128), 0).astype(f32).astype(bf16)

        def tile(i, carry):
            hh = i // 6
            cols = pl.ds(pl.multiple_of((i % 6) * 128, 128), 128)
            acc = jnp.zeros((256, 128), bf16)
            for f in range(FAN):
                row = kf[hh, r * FAN + f:r * FAN + f + 1, cols]
                named = jnp.broadcast_to(row, (16, 128)).astype(bf16)
                named = jnp.concatenate([named] * 16, axis=0)
                acc = acc + jnp.where(rows == named, jnp.ones((), bf16), jnp.zeros((), bf16))
            c_ref[r, pl.ds(pl.multiple_of(hh * 256, 256), 256), cols] = acc
            return carry

        lax.fori_loop(part * 6, part * 6 + 6, tile, 0)

    take_b(1)
    arrive(cp_ax, XN)
    for part in az_parts(1):
        send_a(1, part)
    for t in range(1, 6):
        take_b(t + 1)
        build(t - 1, 0)
        take_a(t)
        build(t - 1, 1)

    arrive(cp_wz, ZN)
    total = wz[z].astype(f32)
    for d in range(1, ZN):
        total = total + wbz[(z + ZN - d) % ZN].astype(f32)
    gz[z] = total.astype(bf16)

    for piece in range(12):
        arrive(lambda d: cp_bx(d, piece), XN)

    def times(r):
        if r < RA:
            m = ma[:, :, :, r * HALF:(r + 1) * HALF]
        else:
            m = mb[:, :, :, (r - RA) * HALF:(r - RA + 1) * HALF]
        return jnp.dot(c_ref[r], m.reshape(XN * ZN * GROUP, HALF), preferred_element_type=f32)

    table = times(3) + times(4)
    take_a(6)
    start(cp_gz, ZN)
    table = table + times(0) + times(1) + times(2)
    for p in range(YN):
        tsend[p] = table[p * 64:(p + 1) * 64].astype(bf16)
    start(cp_t, YN)
    arrive(cp_gz, ZN)
    start(cp_gx, XN)
    arrive(cp_t, YN)
    total = tsend[y].astype(f32)
    for d in range(1, YN):
        total = total + tbuf[(y + YN - d) % YN].astype(f32)
    tall[core, y] = total.astype(bf16)
    start(cp_ta, YN)
    cp_tc(0).start()

    arrive(cp_gx, XN)
    gx[x] = gz[...]
    for p in range(XN):
        for k in range(ZN):
            gout[p * 16:(p + 1) * 16, window_start(k):window_start(k) + GWIN] = gx[p, k]

    def hand_on(d):
        cp_ta(d).wait_recv()
        cp_tc(d).start()

    each(YN, hand_on)
    cp_tc_wait = lambda d: copy(tall.at[other, (y - d + YN) % YN], tall.at[other, (y - d + YN) % YN],
                                s_tc.at[d], r_tc.at[d], partner).wait_recv()
    lax.fori_loop(0, YN, lambda d, carry: (cp_tc_wait(d), carry)[1], 0)
    for c in range(2):
        for p in range(YN):
            tout[p * 64:(p + 1) * 64, c * HALF:(c + 1) * HALF] = tall[c, p]

    def sent(fn, n):
        each(n, lambda d: fn(d).wait_send())

    for r in range(REL):
        cp_w(r).wait_send()
    cp_dp.wait_send()
    sent(cp_kx, XN)
    sent(cp_kz, ZN)
    sent(cp_d, YN)
    sent(cp_wx, XN)
    sent(cp_wz, ZN)
    sent(cp_ax, XN)
    sent(cp_gz, ZN)
    sent(cp_gx, XN)
    sent(cp_t, YN)
    sent(cp_ta, YN)
    lax.fori_loop(0, YN, lambda d, carry: (cp_tc(d).wait_send(), carry)[1], 0)
    for piece in range(12):
        sent(lambda d: cp_bx(d, piece), XN)
    for t in range(1, 7):
        for direction in range(2):
            cp_bz(direction, t).wait_send()
        for part in az_parts(t):
            cp_az(part[0], t, part[1]).wait_send()


def body(agg_rows, seed_feats, seed_type, w_rel, w_self, cotangent, counts, owner, local_row):
    y = lax.axis_index("narrow") // 2
    count = lax.dynamic_slice_in_dim(counts, y * GROUP, GROUP, 0)
    slots = GROUP * REL * FAN
    names = lax.dynamic_slice_in_dim(owner[:, 0], y * slots, slots, 0) * NODES_DEV
    names = names + lax.dynamic_slice_in_dim(local_row, y * slots, slots, 0)
    live = lax.broadcasted_iota(i32, (1, 1, FAN), 2) < count[:, :, None]
    key = jnp.where(live.reshape(GROUP, REL * FAN), names.reshape(GROUP, REL * FAN), -1)
    key = jnp.pad(key, ((0, 0), (0, 128 - REL * FAN)), constant_values=-1)
    cnt = jnp.pad(count.astype(f32), ((0, 0), (0, 128 - REL)), constant_values=1.0)
    vmem = pltpu.VMEM
    dma = lambda n: pltpu.SemaphoreType.DMA((n,))
    one = pltpu.SemaphoreType.DMA
    pairs = lambda *sizes: [dma(n) for n in sizes for _ in range(2)]
    table, grads = pl.pallas_call(
        kernel,
        out_shape=(jax.ShapeDtypeStruct((NODES_DEV, F), bf16), jax.ShapeDtypeStruct((HID, GCOLS), bf16)),
        in_specs=[pl.BlockSpec(memory_space=vmem)] * 8,
        out_specs=(pl.BlockSpec(memory_space=vmem),) * 2,
        scratch_shapes=[
            vmem((HID, REL * HALF), bf16),
            vmem((HID, 128), bf16),
            vmem((HID, 128), bf16),
            vmem((YN, GROUP, REL * HALF), bf16),
            vmem((YN, GROUP, REL * HALF), bf16),
            vmem((ZN, XN, GROUP, 128), i32),
            vmem((2, 128, XN * ZN * GROUP), f32),
            vmem((REL, NODES_DEV, XN * ZN * GROUP), bf16),
            vmem((ZN, XN, GROUP, PA), bf16),
            vmem((ZN, XN, GROUP, PB), bf16),
            vmem((XN, 16, GCOLS), bf16),
            vmem((XN, 16, GCOLS), bf16),
            vmem((ZN, 16, GWIN), bf16),
            vmem((ZN, 16, GWIN), bf16),
            vmem((ZN, 16, GWIN), bf16),
            vmem((XN, ZN, 16, GWIN), bf16),
            vmem((YN, 64, HALF), bf16),
            vmem((YN, 64, HALF), bf16),
            vmem((2, YN, 64, HALF), bf16),
            dma(REL), dma(REL), one, one,
            *pairs(XN, ZN, YN, XN, ZN, XN, 24, 48, 12, ZN, XN, YN, YN, YN),
        ],
        compiler_params=pltpu.CompilerParams(
            collective_id=0, has_side_effects=True, vmem_limit_bytes=56 * 1024 * 1024),
        cost_estimate=pl.CostEstimate(flops=3_500_000_000, bytes_accessed=8_000_000, transcendentals=8192),
    )(agg_rows, w_rel.T, seed_feats, w_self.transpose(0, 2, 1), seed_type.reshape(1, -1), cotangent.T, cnt, key)
    grad_rel = grads[:, :REL * F].astype(f32).T
    grad_self = jnp.stack([grads[:, (REL + t) * F:(REL + t + 1) * F].astype(f32).T for t in range(2)])
    return table.astype(f32), grad_rel, grad_self


def solution(mesh):
    in_specs = (
        P("wide", None),
        P("wide", None),
        P("wide"),
        P(None, "narrow"),
        P(None, None, "narrow"),
        P("wide", "narrow"),
        P("wide", None),
        P("wide", None),
        P("wide"),
    )
    out_specs = (P("wide", None), P(None, "narrow"), P(None, None, "narrow"))
    return jax.shard_map(body, mesh=mesh, in_specs=in_specs, out_specs=out_specs, check_vma=False)
```

```python
import jax
import jax.numpy as jnp
from jax import lax
from jax.experimental import pallas as pl
from jax.experimental.pallas import tpu as pltpu
from jax.sharding import PartitionSpec as P

FAN = 25
NODES_DEV = 512
REL = 5
F = 768
HALF = 384
HID = 64
XN, ZN, YN = 4, 12, 8
GROUP = 16
ROWS = XN * ZN * GROUP
ALLH = 2 * YN * HID
SHARE = 256
PLAIN = REL * HALF - XN * SHARE
GCOLS = REL * F + 2 * F
GWIN = 512
DEAD = 32767
MESH = pl.DeviceIdType.MESH
f32, bf16, i32 = jnp.float32, jnp.bfloat16, jnp.int32


def window_start(k):
    return 128 * ((7 * k) // 2)


def kernel(agg, wr, seeds, ws, kind, cot, key, tout, gout,
           wnat, wy, wsh, dsend, dbuf, d_all, m_ref, inv, kall, kf, c_ref,
           wx, wbx, wz, wbz, gz, gx, tsend, tbuf, tall,
           s_w, r_w, s_kx, r_kx, s_kz, r_kz, s_kp, r_kp, s_d, r_d, s_wx, r_wx, s_wz, r_wz,
           s_wr, r_wr, s_sx, r_sx, s_dx, r_dx, s_px, r_px, s_d1, r_d1, s_dz, r_dz, s_pz, r_pz,
           s_gz, r_gz, s_gx, r_gx, s_t, r_t, s_ta, r_ta, s_tc, r_tc):
    wide, narrow = lax.axis_index("wide"), lax.axis_index("narrow")
    x, z = wide // ZN, wide % ZN
    y, core = narrow // 2, narrow % 2
    other = 1 - core

    def at_x(p):
        return (p * ZN + z, narrow)

    def at_z(p):
        return (x * ZN + p, narrow)

    def at_y(p):
        return (wide, p * 2 + core)

    partner = (wide, y * 2 + other)

    def at_xz(p, q):
        return (p * ZN + q, narrow)

    def copy(src, dst, s, r, to):
        return pltpu.make_async_remote_copy(
            src_ref=src, dst_ref=dst, send_sem=s, recv_sem=r, device_id=to, device_id_type=MESH)

    barrier = pltpu.get_barrier_semaphore()

    def greet(to):
        pl.semaphore_signal(barrier, inc=1, device_id=to, device_id_type=MESH)

    def each(n, fn, low=1):
        def step(d, carry):
            fn(d)
            return carry
        lax.fori_loop(low, n, step, 0)

    each(XN, lambda d: greet(at_x((x + d) % XN)))
    each(ZN, lambda d: greet(at_z((z + d) % ZN)))
    each(YN, lambda d: greet(at_y((y + d) % YN)))
    greet(partner)
    for step in (1, ZN - 1):
        each(XN, lambda d: greet(at_xz((x + d) % XN, (z + step) % ZN)))
    pl.semaphore_wait(barrier, 3 * XN + ZN + YN - 4)

    pending = []

    def start(fn, n):
        pending.append((fn, n))
        each(n, lambda d: fn(d).start())

    def start1(cp):
        pending.append((lambda d: cp, 2))
        cp.start()

    def arrive(fn, n):
        each(n, lambda d: fn(d).wait_recv())

    def cp_w(r):
        cols = pl.ds(pl.multiple_of(r * F + other * HALF, 128), HALF)
        return copy(wr.at[:, cols], wnat.at[core, :, pl.ds(r * HALF, HALF)], s_w.at[r], r_w.at[r], partner)

    def cp_kx(d):
        return copy(kall.at[z, x], kall.at[z, x], s_kx.at[d], r_kx.at[d], at_x((x + d) % XN))

    mine_x = pl.ds(2 * core, 2)

    def cp_kz(d):
        part = kall.at[z, mine_x]
        return copy(part, part, s_kz.at[d], r_kz.at[d], at_z((z + d) % ZN))

    def cp_kp(d):
        part = kall.at[(z - d + ZN) % ZN, mine_x]
        return copy(part, part, s_kp.at[d], r_kp.at[d], partner)

    def cp_d(d):
        p = (y + d) % YN
        return copy(dsend.at[p], dbuf.at[y], s_d.at[d], r_d.at[d], at_y(p))

    def cp_wx(d):
        p = (x + d) % XN
        return copy(wx.at[p], wbx.at[x], s_wx.at[d], r_wx.at[d], at_x(p))

    def cp_wz(d):
        p = (z + d) % ZN
        return copy(wz.at[p], wbz.at[z], s_wz.at[d], r_wz.at[d], at_z(p))

    def cp_gz(d):
        return copy(gz.at[z], gz.at[z], s_gz.at[d], r_gz.at[d], at_z((z + d) % ZN))

    def cp_gx(d):
        return copy(gz, gx.at[x], s_gx.at[d], r_gx.at[d], at_x((x + d) % XN))

    def cp_t(d):
        p = (y + d) % YN
        return copy(tsend.at[p], tbuf.at[y], s_t.at[d], r_t.at[d], at_y(p))

    def cp_tc(d, c=None):
        part = tall.at[core if c is None else c, (y - d + YN) % YN]
        return copy(part, part, s_tc.at[d], r_tc.at[d], partner)

    def held_y(direction, t):
        return (y - (t - 1) + YN) % YN if direction == 0 else (y + (t - 1)) % YN

    def next_y(direction):
        return at_y((y + 1) % YN if direction == 0 else (y + YN - 1) % YN)

    def cp_wr(direction, t, j):
        p, c = held_y(direction, t), core if j % 2 == 0 else other
        part = wy.at[c, p] if j < 2 else wsh.at[x, c, p]
        i = (direction * 4 + t - 1) * 4 + j
        return copy(part, part, s_wr.at[i], r_wr.at[i], next_y(direction))

    def send_w(t, j):
        for direction in range(2):
            if t < 4 or j % 2 == direction:
                start1(cp_wr(direction, t, j))

    def take_w(t, j):
        for direction in range(2):
            if t == 4 and j % 2 != direction:
                continue
            cp_wr(direction, t, j).wait_recv()
            if t < 3 or (t == 3 and j % 2 == direction):
                start1(cp_wr(direction, t + 1, j))
            if j == 3 and t < 4:
                start(lambda d, piece=direction * 3 + t - 1: cp_sx(d, piece), XN)
            if j == 3 and t == 4:
                start(lambda d: cp_sx(d, 6), XN)

    def take_all(t):
        for j in (2, 0, 3, 1):
            take_w(t, j)

    def cp_ta(d):
        return copy(tall.at[core, y], tall.at[core, y], s_ta.at[d], r_ta.at[d], at_y((y + d) % YN))

    def piece_y(piece):
        return (y - piece - 1 + YN) % YN if piece < 3 else (y + piece - 2) % YN if piece < 6 else (y + 4) % YN

    def cp_sx(d, piece):
        part = wsh.at[x, :, piece_y(piece)]
        i = piece * XN + d
        return copy(part, part, s_sx.at[i], r_sx.at[i], at_x((x + d) % XN))

    half = pl.ds(pl.multiple_of(core * (ALLH // 2), 128), ALLH // 2)

    def cp_dx(d):
        part = d_all.at[z, x, :, half]
        return copy(part, part, s_dx.at[d], r_dx.at[d], at_x((x + d) % XN))

    def cp_px(d):
        part = d_all.at[z, (x - d + XN) % XN, :, half]
        return copy(part, part, s_px.at[d], r_px.at[d], partner)

    def held(direction, t):
        return (z - (t - 1) + ZN) % ZN if direction == 0 else (z + (t - 1)) % ZN

    def next_z(direction):
        return at_z((z + 1) % ZN if direction == 0 else (z + ZN - 1) % ZN)

    def cp_dz(direction, t, h):
        part = d_all.at[held(direction, t), pl.ds(2 * h, 2), :, half]
        i = (direction * 6 + t - 1) * 2 + h
        return copy(part, part, s_dz.at[i], r_dz.at[i], next_z(direction))

    def cp_pz(direction, t):
        p = (z - t + ZN) % ZN if direction == 0 else (z + t) % ZN
        part = d_all.at[p, :, :, half]
        i = direction * 6 + t - 1
        return copy(part, part, s_pz.at[i], r_pz.at[i], partner)

    def cp_d1(direction, d):
        part = d_all.at[z, x, :, half]
        i = direction * XN + d
        to = at_xz((x + d) % XN, (z + 1) % ZN if direction == 0 else (z + ZN - 1) % ZN)
        return copy(part, part, s_d1.at[i], r_d1.at[i], to)

    def dz_parts(t):
        return [(0, 0), (1, 0), (0, 1), (1, 1)] if t < 6 else [(0, 0), (1, 1)]

    for r in range(REL):
        start1(cp_w(r))
    kall[z, x] = jnp.full((8, 128), DEAD * 65537, i32)
    kall[z, x, :, 0:REL * FAN] = key[...]
    start(cp_kx, XN)

    contract = (((1,), (1,)), ((), ()))
    zero = lax.dot_general(ws[0], seeds[...], contract, preferred_element_type=f32)
    one = lax.dot_general(ws[1], seeds[...], contract, preferred_element_type=f32)
    first = kind[...] == 0
    pre = jnp.where(first, zero, one)
    pre = pre + lax.dot_general(wr[...], agg[...], contract, preferred_element_type=f32)
    sigma = 1.0 / (1.0 + jnp.exp(-pre))
    dpre_b = (cot[...] * sigma * (1.0 + pre * (1.0 - sigma))).astype(bf16)

    wide_rows = jnp.concatenate([dpre_b.astype(f32), jnp.zeros((128 - HID, 128), f32)], axis=0)
    wide_rows = wide_rows.T.astype(bf16)
    for p in range(YN):
        dsend[p] = wide_rows[p * GROUP:(p + 1) * GROUP]
    start(cp_d, YN)
    dbuf[y] = dsend[y]

    def place_w(c):
        wy[c, y] = wnat[c, :, 0:PLAIN]
        for p in range(XN):
            wsh[p, c, y] = wnat[c, :, PLAIN + p * SHARE:PLAIN + (p + 1) * SHARE]

    for r in range(REL):
        cols = pl.ds(pl.multiple_of(r * F + core * HALF, 128), HALF)
        wnat[core, :, r * HALF:(r + 1) * HALF] = wr[:, cols]
    place_w(core)
    send_w(1, 2)
    send_w(1, 0)
    for r in range(REL):
        cp_w(r).wait_recv()
    place_w(other)
    send_w(1, 3)
    send_w(1, 1)
    arrive(cp_kx, XN)
    start(cp_kz, ZN)

    def grads(low, high):
        for r in range(low, high):
            if r < REL:
                g = jnp.dot(dpre_b, agg[:, r * F:(r + 1) * F], preferred_element_type=f32)
            else:
                mask = first if r == REL else jnp.logical_not(first)
                part = jnp.where(mask, dpre_b.astype(f32), 0.0).astype(bf16)
                g = jnp.dot(part, seeds[...], preferred_element_type=f32)
            g = g.astype(bf16)
            for p in range(XN):
                wx[p, :, r * F:(r + 1) * F] = g[p * 16:(p + 1) * 16]

    grads(0, 5)
    arrive(cp_d, YN)
    block = jnp.concatenate([dbuf[2 * p][:, 0:HID].astype(f32) if c == 0 else dbuf[2 * p + 1][:, 0:HID].astype(f32)
                             for p in range(YN // 2) for c in range(2)], axis=1).astype(bf16)
    d_all[z, x, :, half] = block
    for direction in range(2):
        pending.append((lambda d, direction=direction: cp_d1(direction, d - 1), XN + 1))
        each(XN, lambda d: cp_d1(direction, d).start(), 0)
    start(cp_dx, XN)
    grads(5, 7)
    pending.append((lambda d: cp_px(d - 1), XN + 1))
    cp_px(0).start()
    take_w(1, 2)

    def take_d(t):
        if t == 1:
            for direction in range(2):
                each(XN, lambda d: cp_d1(direction, d).wait_recv(), 0)
                for h in range(2):
                    start1(cp_dz(direction, 2, h))
                start1(cp_pz(direction, 1))
            return
        for part in dz_parts(t):
            cp_dz(part[0], t, part[1]).wait_recv()
            if t < 6 and part in dz_parts(t + 1):
                start1(cp_dz(part[0], t + 1, part[1]))
            if t < 6 and part[1] == 1:
                start1(cp_pz(part[0], t))
        if t == 6:
            start1(cp_pz(0, 6))

    def build(r):
        rows = lax.broadcasted_iota(i32, (256, 128), 0).astype(f32).astype(bf16)

        def tile(i, carry):
            hh = i // 6
            cols = pl.ds(pl.multiple_of((i % 6) * 128, 128), 128)
            acc = jnp.zeros((256, 128), bf16)
            for f in range(FAN):
                row = kf[hh, r * FAN + f:r * FAN + f + 1, cols]
                named = jnp.broadcast_to(row, (16, 128)).astype(bf16)
                named = jnp.concatenate([named] * 16, axis=0)
                acc = acc + jnp.where(rows == named, jnp.ones((), bf16), jnp.zeros((), bf16))
            c_ref[r, pl.ds(pl.multiple_of(hh * 256, 256), 256), cols] = acc
            return carry

        lax.fori_loop(0, 12, tile, 0)

    def hand_keys():
        pending.append((cp_kp, ZN))

        def hand(d):
            cp_kz(d).wait_recv()
            cp_kp(d).start()

        each(ZN, hand)

    def read_keys():
        arrive(cp_kp, ZN)
        packed = kall[...]
        keys = jnp.concatenate([packed % 65536, packed // 65536], axis=2).reshape(ROWS, 128)
        lane = lax.broadcasted_iota(i32, (ROWS, 128), 1)
        live = keys != DEAD
        for r in range(REL):
            mine = jnp.logical_and(live, jnp.logical_and(lane >= r * FAN, lane < (r + 1) * FAN))
            count = jnp.sum(jnp.where(mine, 1.0, 0.0), axis=1, keepdims=True)
            inv[r] = jnp.broadcast_to(1.0 / count, (ROWS, 128))
        keys = keys.astype(f32).T
        base = (wide * NODES_DEV).astype(f32)
        for hh in range(2):
            v = keys - (base + 256.0 * hh)
            kf[hh] = jnp.where((v >= 0.0) & (v < 256.0), v, -1.0)

    def sum_x():
        arrive(cp_wx, XN)
        for r in range(7):
            cols = slice(r * F, (r + 1) * F)
            total = wx[x, :, cols].astype(f32)
            for d in range(1, XN):
                total = total + wbx[(x + XN - d) % XN, :, cols].astype(f32)
            wx[x, :, cols] = total.astype(bf16)
        for k in range(ZN):
            wz[k] = wx[x, :, window_start(k):window_start(k) + GWIN]
        start(cp_wz, ZN)

    def multiply(cols, weights):
        out = jnp.dot(d_all[...].reshape(ROWS, ALLH), weights, preferred_element_type=f32)
        for low in range(cols.start, cols.stop, 128):
            m_ref[:, low:low + 128] = (out[:, low - cols.start:low - cols.start + 128] * inv[low // HALF]).astype(bf16)

    def shares(pieces):
        for piece in pieces:
            arrive(lambda d: cp_sx(d, piece), XN)

    hand_keys()
    take_w(1, 0)
    take_d(1)
    arrive(cp_dx, XN)
    each(XN, lambda d: cp_px(d).start())
    take_w(1, 3)
    take_w(1, 1)
    read_keys()
    take_d(2)
    build(0)
    take_d(3)
    take_w(2, 2)
    take_w(2, 0)
    build(1)
    take_d(4)
    take_w(2, 3)
    take_w(2, 1)
    build(2)
    take_d(5)
    start(cp_wx, XN)
    build(3)
    take_d(6)
    take_w(3, 2)
    take_w(3, 0)
    take_w(3, 3)
    take_w(3, 1)
    build(4)
    each(XN, lambda d: cp_px(d).wait_recv(), 0)
    for t in range(1, 6):
        for direction in range(2):
            cp_pz(direction, t).wait_recv()
    cp_pz(0, 6).wait_recv()
    take_w(4, 2)
    take_w(4, 3)
    take_w(4, 0)
    take_w(4, 1)
    sum_x()
    multiply(slice(0, 512), wy[:, :, :, 0:512].reshape(ALLH, 512))
    multiply(slice(512, PLAIN), wy[:, :, :, 512:PLAIN].reshape(ALLH, PLAIN - 512))
    shares(range(7))
    for p in range(XN):
        low = PLAIN + p * SHARE
        multiply(slice(low, low + SHARE), wsh[p].reshape(ALLH, SHARE))

    table = None
    for r in range(REL):
        out = jnp.dot(c_ref[r], m_ref[:, r * HALF:(r + 1) * HALF], preferred_element_type=f32)
        table = out if table is None else table + out
    for p in range(YN):
        tsend[p] = table[p * 64:(p + 1) * 64].astype(bf16)
    start(cp_t, YN)

    arrive(cp_wz, ZN)
    total = wz[z].astype(f32)
    for d in range(1, ZN):
        total = total + wbz[(z + ZN - d) % ZN].astype(f32)
    gz[z] = total.astype(bf16)
    start(cp_gz, ZN)

    arrive(cp_t, YN)
    total = tsend[y].astype(f32)
    for d in range(1, YN):
        total = total + tbuf[(y + YN - d) % YN].astype(f32)
    tall[core, y] = total.astype(bf16)
    start(cp_ta, YN)
    start1(cp_tc(0))
    arrive(cp_gz, ZN)
    start(cp_gx, XN)

    def hand_on(d):
        cp_ta(d).wait_recv()
        cp_tc(d).start()

    each(YN, hand_on)
    pending.append((cp_tc, YN))
    arrive(cp_gx, XN)
    gx[x] = gz[...]
    for p in range(XN):
        for k in range(ZN):
            gout[p * 16:(p + 1) * 16, window_start(k):window_start(k) + GWIN] = gx[p, k]

    each(YN, lambda d: cp_tc(d, other).wait_recv(), 0)
    for c in range(2):
        for p in range(YN):
            tout[p * 64:(p + 1) * 64, c * HALF:(c + 1) * HALF] = tall[c, p]

    for fn, n in pending:
        each(n, lambda d: fn(d).wait_send())


def body(agg_rows, seed_feats, seed_type, w_rel, w_self, cotangent, counts, owner, local_row):
    y = lax.axis_index("narrow") // 2
    count = lax.dynamic_slice_in_dim(counts, y * GROUP, GROUP, 0)
    slots = GROUP * REL * FAN
    names = lax.dynamic_slice_in_dim(owner[:, 0] * NODES_DEV + local_row, y * slots, slots, 0)
    live = lax.broadcasted_iota(i32, (1, 1, FAN), 2) < count[:, :, None]
    key = jnp.where(live.reshape(GROUP, REL * FAN), names.reshape(GROUP, REL * FAN), DEAD)
    key = key[:8] + key[8:] * 65536
    vmem = pltpu.VMEM
    dma = lambda n: pltpu.SemaphoreType.DMA((n,))
    pairs = lambda *sizes: [dma(n) for n in sizes for _ in range(2)]
    table, grads = pl.pallas_call(
        kernel,
        out_shape=(jax.ShapeDtypeStruct((NODES_DEV, F), bf16), jax.ShapeDtypeStruct((HID, GCOLS), bf16)),
        in_specs=[pl.BlockSpec(memory_space=vmem)] * 7,
        out_specs=(pl.BlockSpec(memory_space=vmem),) * 2,
        scratch_shapes=[
            vmem((2, HID, REL * HALF), bf16),
            vmem((2, YN, HID, PLAIN), bf16),
            vmem((XN, 2, YN, HID, SHARE), bf16),
            vmem((YN, GROUP, 128), bf16),
            vmem((YN, GROUP, 128), bf16),
            vmem((ZN, XN, GROUP, ALLH), bf16),
            vmem((ROWS, REL * HALF), bf16),
            vmem((REL, ROWS, 128), f32),
            vmem((ZN, XN, 8, 128), i32),
            vmem((2, 128, ROWS), f32),
            vmem((REL, NODES_DEV, ROWS), bf16),
            vmem((XN, 16, GCOLS), bf16),
            vmem((XN, 16, GCOLS), bf16),
            vmem((ZN, 16, GWIN), bf16),
            vmem((ZN, 16, GWIN), bf16),
            vmem((ZN, 16, GWIN), bf16),
            vmem((XN, ZN, 16, GWIN), bf16),
            vmem((YN, 64, HALF), bf16),
            vmem((YN, 64, HALF), bf16),
            vmem((2, YN, 64, HALF), bf16),
            *pairs(REL, XN, ZN, ZN, YN, XN, ZN, 32, 28, XN, XN, 8, 24, 12, ZN, XN, YN, YN, YN),
        ],
        compiler_params=pltpu.CompilerParams(
            collective_id=0, has_side_effects=True, vmem_limit_bytes=56 * 1024 * 1024),
        cost_estimate=pl.CostEstimate(flops=6_500_000_000, bytes_accessed=8_000_000, transcendentals=8192),
    )(agg_rows, w_rel.T, seed_feats, w_self.transpose(0, 2, 1), seed_type.reshape(1, -1), cotangent.T, key)
    grad_rel = grads[:, :REL * F].astype(f32).T
    grad_self = jnp.stack([grads[:, (REL + t) * F:(REL + t + 1) * F].astype(f32).T for t in range(2)])
    return table.astype(f32), grad_rel, grad_self


def solution(mesh):
    in_specs = (
        P("wide", None),
        P("wide", None),
        P("wide"),
        P(None, "narrow"),
        P(None, None, "narrow"),
        P("wide", "narrow"),
        P("wide", None),
        P("wide", None),
        P("wide"),
    )
    out_specs = (P("wide", None), P(None, "narrow"), P(None, None, "narrow"))
    return jax.shard_map(body, mesh=mesh, in_specs=in_specs, out_specs=out_specs, check_vma=False)
```

```python
import jax
import jax.numpy as jnp
from jax import lax
from jax.experimental import pallas as pl
from jax.experimental.pallas import tpu as pltpu
from jax.sharding import PartitionSpec as P

FAN = 25
NODES_DEV = 512
REL = 5
F = 768
HALF = 384
HID = 64
XN, ZN, YN = 4, 12, 8
GROUP = 16
ROWS = XN * ZN * GROUP
ALLH = 2 * YN * HID
SHARE = 256
PLAIN = REL * HALF - XN * SHARE
GCOLS = REL * F + 2 * F
GWIN = 512
DEAD = 32767
MESH = pl.DeviceIdType.MESH
f32, bf16, i32 = jnp.float32, jnp.bfloat16, jnp.int32


def window_start(k):
    return 128 * ((7 * k) // 2)


def kernel(agg, wr, seeds, ws, kind, cot, key, tout, gout,
           wnat, wy, wsh, dsend, dbuf, d_all, m_ref, inv, kall, kf, c_ref,
           wx, wbx, wz, wbz, gz, gx, tsend, tbuf, tall,
           s_w, r_w, s_kx, r_kx, s_kz, r_kz, s_kp, r_kp, s_d, r_d, s_wx, r_wx, s_wz, r_wz,
           s_wr, r_wr, s_sx, r_sx, s_dx, r_dx, s_px, r_px, s_d1, r_d1, s_dz, r_dz, s_pz, r_pz,
           s_gz, r_gz, s_gx, r_gx, s_t, r_t, s_ta, r_ta, s_tc, r_tc):
    wide, narrow = lax.axis_index("wide"), lax.axis_index("narrow")
    x, z = wide // ZN, wide % ZN
    y, core = narrow // 2, narrow % 2
    other = 1 - core

    def at_x(p):
        return (p * ZN + z, narrow)

    def at_z(p):
        return (x * ZN + p, narrow)

    def at_y(p):
        return (wide, p * 2 + core)

    partner = (wide, y * 2 + other)

    def at_xz(p, q):
        return (p * ZN + q, narrow)

    def copy(src, dst, s, r, to):
        return pltpu.make_async_remote_copy(
            src_ref=src, dst_ref=dst, send_sem=s, recv_sem=r, device_id=to, device_id_type=MESH)

    barrier = pltpu.get_barrier_semaphore()

    def greet(to):
        pl.semaphore_signal(barrier, inc=1, device_id=to, device_id_type=MESH)

    def each(n, fn, low=1):
        def step(d, carry):
            fn(d)
            return carry
        lax.fori_loop(low, n, step, 0)

    each(XN, lambda d: greet(at_x((x + d) % XN)))
    each(ZN, lambda d: greet(at_z((z + d) % ZN)))
    each(YN, lambda d: greet(at_y((y + d) % YN)))
    greet(partner)
    for step in (1, ZN - 1):
        each(XN, lambda d: greet(at_xz((x + d) % XN, (z + step) % ZN)))
    pl.semaphore_wait(barrier, 3 * XN + ZN + YN - 4)

    pending = []

    def start(fn, n):
        pending.append((fn, n))
        each(n, lambda d: fn(d).start())

    def start1(cp):
        pending.append((lambda d: cp, 2))
        cp.start()

    def arrive(fn, n):
        each(n, lambda d: fn(d).wait_recv())

    def cp_w(r):
        cols = pl.ds(pl.multiple_of(r * F + other * HALF, 128), HALF)
        return copy(wr.at[:, cols], wnat.at[core, :, pl.ds(r * HALF, HALF)], s_w.at[r], r_w.at[r], partner)

    def cp_kx(d):
        return copy(kall.at[z, x], kall.at[z, x], s_kx.at[d], r_kx.at[d], at_x((x + d) % XN))

    mine_x = pl.ds(2 * core, 2)

    def cp_kz(d):
        part = kall.at[z, mine_x]
        return copy(part, part, s_kz.at[d], r_kz.at[d], at_z((z + d) % ZN))

    def cp_kp(d):
        part = kall.at[(z - d + ZN) % ZN, mine_x]
        return copy(part, part, s_kp.at[d], r_kp.at[d], partner)

    def cp_d(d):
        p = (y + d) % YN
        return copy(dsend.at[p], dbuf.at[y], s_d.at[d], r_d.at[d], at_y(p))

    def cp_wx(d):
        p = (x + d) % XN
        return copy(wx.at[p], wbx.at[x], s_wx.at[d], r_wx.at[d], at_x(p))

    def cp_wz(d):
        p = (z + d) % ZN
        return copy(wz.at[p], wbz.at[z], s_wz.at[d], r_wz.at[d], at_z(p))

    def cp_gz(d):
        return copy(gz.at[z], gz.at[z], s_gz.at[d], r_gz.at[d], at_z((z + d) % ZN))

    def cp_gx(d):
        return copy(gz, gx.at[x], s_gx.at[d], r_gx.at[d], at_x((x + d) % XN))

    def part_rows(h):
        return pl.ds(32 * h, 32)

    def cp_t(d, h):
        p = (y + d) % YN
        i = h * YN + d
        return copy(tsend.at[p, part_rows(h)], tbuf.at[y, part_rows(h)], s_t.at[i], r_t.at[i], at_y(p))

    def cp_tc(d, h, c=None):
        part = tall.at[core if c is None else c, (y - d + YN) % YN, part_rows(h)]
        i = h * YN + d
        return copy(part, part, s_tc.at[i], r_tc.at[i], partner)

    def held_y(direction, t):
        return (y - (t - 1) + YN) % YN if direction == 0 else (y + (t - 1)) % YN

    def next_y(direction):
        return at_y((y + 1) % YN if direction == 0 else (y + YN - 1) % YN)

    def cp_wr(direction, t, j):
        p, c = held_y(direction, t), core if j % 2 == 0 else other
        part = wy.at[c, p] if j < 2 else wsh.at[x, c, p]
        i = (direction * 4 + t - 1) * 4 + j
        return copy(part, part, s_wr.at[i], r_wr.at[i], next_y(direction))

    def send_w(t, j):
        for direction in range(2):
            if t < 4 or j % 2 == direction:
                start1(cp_wr(direction, t, j))

    def take_w(t, j):
        for direction in range(2):
            if t == 4 and j % 2 != direction:
                continue
            cp_wr(direction, t, j).wait_recv()
            if t < 3 or (t == 3 and j % 2 == direction):
                start1(cp_wr(direction, t + 1, j))
            if j == 3 and t < 4:
                start(lambda d, piece=direction * 3 + t - 1: cp_sx(d, piece), XN)
            if j == 3 and t == 4:
                start(lambda d: cp_sx(d, 6), XN)

    def take_all(t):
        for j in (2, 0, 3, 1):
            take_w(t, j)

    def cp_ta(d, h):
        part = tall.at[core, y, part_rows(h)]
        i = h * YN + d
        return copy(part, part, s_ta.at[i], r_ta.at[i], at_y((y + d) % YN))

    def piece_y(piece):
        return (y - piece - 1 + YN) % YN if piece < 3 else (y + piece - 2) % YN if piece < 6 else (y + 4) % YN

    def cp_sx(d, piece):
        part = wsh.at[x, :, piece_y(piece)]
        i = piece * XN + d
        return copy(part, part, s_sx.at[i], r_sx.at[i], at_x((x + d) % XN))

    half = pl.ds(pl.multiple_of(core * (ALLH // 2), 128), ALLH // 2)

    def cp_dx(d):
        part = d_all.at[z, x, :, half]
        return copy(part, part, s_dx.at[d], r_dx.at[d], at_x((x + d) % XN))

    def cp_px(d):
        part = d_all.at[z, (x - d + XN) % XN, :, half]
        return copy(part, part, s_px.at[d], r_px.at[d], partner)

    def held(direction, t):
        return (z - (t - 1) + ZN) % ZN if direction == 0 else (z + (t - 1)) % ZN

    def next_z(direction):
        return at_z((z + 1) % ZN if direction == 0 else (z + ZN - 1) % ZN)

    def cp_dz(direction, t, h):
        part = d_all.at[held(direction, t), pl.ds(2 * h, 2), :, half]
        i = (direction * 6 + t - 1) * 2 + h
        return copy(part, part, s_dz.at[i], r_dz.at[i], next_z(direction))

    def cp_pz(direction, t):
        p = (z - t + ZN) % ZN if direction == 0 else (z + t) % ZN
        part = d_all.at[p, :, :, half]
        i = direction * 6 + t - 1
        return copy(part, part, s_pz.at[i], r_pz.at[i], partner)

    def cp_d1(direction, d):
        part = d_all.at[z, x, :, half]
        i = direction * XN + d
        to = at_xz((x + d) % XN, (z + 1) % ZN if direction == 0 else (z + ZN - 1) % ZN)
        return copy(part, part, s_d1.at[i], r_d1.at[i], to)

    def dz_parts(t):
        return [(0, 0), (1, 0), (0, 1), (1, 1)] if t < 6 else [(0, 0), (1, 1)]

    for r in range(REL):
        start1(cp_w(r))
    kall[z, x] = jnp.full((8, 128), DEAD * 65537, i32)
    kall[z, x, :, 0:REL * FAN] = key[...]
    start(cp_kx, XN)

    contract = (((1,), (1,)), ((), ()))
    zero = lax.dot_general(ws[0], seeds[...], contract, preferred_element_type=f32)
    one = lax.dot_general(ws[1], seeds[...], contract, preferred_element_type=f32)
    first = kind[...] == 0
    pre = jnp.where(first, zero, one)
    pre = pre + lax.dot_general(wr[...], agg[...], contract, preferred_element_type=f32)
    sigma = 1.0 / (1.0 + jnp.exp(-pre))
    dpre_b = (cot[...] * sigma * (1.0 + pre * (1.0 - sigma))).astype(bf16)

    wide_rows = jnp.concatenate([dpre_b.astype(f32), jnp.zeros((128 - HID, 128), f32)], axis=0)
    wide_rows = wide_rows.T.astype(bf16)
    for p in range(YN):
        dsend[p] = wide_rows[p * GROUP:(p + 1) * GROUP]
    start(cp_d, YN)
    dbuf[y] = dsend[y]

    def place_w(c):
        wy[c, y] = wnat[c, :, 0:PLAIN]
        for p in range(XN):
            wsh[p, c, y] = wnat[c, :, PLAIN + p * SHARE:PLAIN + (p + 1) * SHARE]

    for r in range(REL):
        cols = pl.ds(pl.multiple_of(r * F + core * HALF, 128), HALF)
        wnat[core, :, r * HALF:(r + 1) * HALF] = wr[:, cols]
    place_w(core)
    send_w(1, 2)
    send_w(1, 0)
    for r in range(REL):
        cp_w(r).wait_recv()
    place_w(other)
    send_w(1, 3)
    send_w(1, 1)
    arrive(cp_kx, XN)
    start(cp_kz, ZN)

    def grads(low, high):
        for r in range(low, high):
            if r < REL:
                g = jnp.dot(dpre_b, agg[:, r * F:(r + 1) * F], preferred_element_type=f32)
            else:
                mask = first if r == REL else jnp.logical_not(first)
                part = jnp.where(mask, dpre_b.astype(f32), 0.0).astype(bf16)
                g = jnp.dot(part, seeds[...], preferred_element_type=f32)
            g = g.astype(bf16)
            for p in range(XN):
                wx[p, :, r * F:(r + 1) * F] = g[p * 16:(p + 1) * 16]

    grads(0, 5)
    arrive(cp_d, YN)
    block = jnp.concatenate([dbuf[2 * p][:, 0:HID].astype(f32) if c == 0 else dbuf[2 * p + 1][:, 0:HID].astype(f32)
                             for p in range(YN // 2) for c in range(2)], axis=1).astype(bf16)
    d_all[z, x, :, half] = block
    for direction in range(2):
        pending.append((lambda d, direction=direction: cp_d1(direction, d - 1), XN + 1))
        each(XN, lambda d: cp_d1(direction, d).start(), 0)
    start(cp_dx, XN)
    grads(5, 7)
    pending.append((lambda d: cp_px(d - 1), XN + 1))
    cp_px(0).start()
    take_w(1, 2)

    def take_d(t):
        if t == 1:
            for direction in range(2):
                each(XN, lambda d: cp_d1(direction, d).wait_recv(), 0)
                for h in range(2):
                    start1(cp_dz(direction, 2, h))
                start1(cp_pz(direction, 1))
            return
        for part in dz_parts(t):
            cp_dz(part[0], t, part[1]).wait_recv()
            if t < 6 and part in dz_parts(t + 1):
                start1(cp_dz(part[0], t + 1, part[1]))
            if t < 6 and part[1] == 1:
                start1(cp_pz(part[0], t))
        if t == 6:
            start1(cp_pz(0, 6))

    def build(r):
        rows = lax.broadcasted_iota(i32, (256, 128), 0).astype(f32).astype(bf16)

        def tile(i, carry):
            hh = i // 6
            cols = pl.ds(pl.multiple_of((i % 6) * 128, 128), 128)
            acc = jnp.zeros((256, 128), bf16)
            for f in range(FAN):
                row = kf[hh, r * FAN + f:r * FAN + f + 1, cols]
                named = jnp.broadcast_to(row, (16, 128)).astype(bf16)
                named = jnp.concatenate([named] * 16, axis=0)
                acc = acc + jnp.where(rows == named, jnp.ones((), bf16), jnp.zeros((), bf16))
            c_ref[r, pl.ds(pl.multiple_of(hh * 256, 256), 256), cols] = acc
            return carry

        lax.fori_loop(0, 12, tile, 0)

    def hand_keys():
        pending.append((cp_kp, ZN))

        def hand(d):
            cp_kz(d).wait_recv()
            cp_kp(d).start()

        each(ZN, hand)

    def read_keys():
        arrive(cp_kp, ZN)
        packed = kall[...]
        keys = jnp.concatenate([packed % 65536, packed // 65536], axis=2).reshape(ROWS, 128)
        lane = lax.broadcasted_iota(i32, (ROWS, 128), 1)
        live = keys != DEAD
        for r in range(REL):
            mine = jnp.logical_and(live, jnp.logical_and(lane >= r * FAN, lane < (r + 1) * FAN))
            count = jnp.sum(jnp.where(mine, 1.0, 0.0), axis=1, keepdims=True)
            inv[r] = jnp.broadcast_to(1.0 / count, (ROWS, 128))
        keys = keys.astype(f32).T
        base = (wide * NODES_DEV).astype(f32)
        for hh in range(2):
            v = keys - (base + 256.0 * hh)
            kf[hh] = jnp.where((v >= 0.0) & (v < 256.0), v, -1.0)

    def sum_x():
        arrive(cp_wx, XN)
        for r in range(7):
            cols = slice(r * F, (r + 1) * F)
            total = wx[x, :, cols].astype(f32)
            for d in range(1, XN):
                total = total + wbx[(x + XN - d) % XN, :, cols].astype(f32)
            wx[x, :, cols] = total.astype(bf16)
        for k in range(ZN):
            wz[k] = wx[x, :, window_start(k):window_start(k) + GWIN]
        start(cp_wz, ZN)

    def multiply(cols, weights):
        out = jnp.dot(d_all[...].reshape(ROWS, ALLH), weights, preferred_element_type=f32)
        for low in range(cols.start, cols.stop, 128):
            m_ref[:, low:low + 128] = (out[:, low - cols.start:low - cols.start + 128] * inv[low // HALF]).astype(bf16)

    def shares(pieces):
        for piece in pieces:
            arrive(lambda d: cp_sx(d, piece), XN)

    hand_keys()
    take_w(1, 0)
    take_d(1)
    arrive(cp_dx, XN)
    each(XN, lambda d: cp_px(d).start())
    take_w(1, 3)
    take_w(1, 1)
    read_keys()
    take_d(2)
    build(0)
    take_d(3)
    take_w(2, 2)
    take_w(2, 0)
    build(1)
    take_d(4)
    take_w(2, 3)
    take_w(2, 1)
    build(2)
    take_d(5)
    start(cp_wx, XN)
    build(3)
    take_d(6)
    take_w(3, 2)
    take_w(3, 0)
    take_w(3, 3)
    take_w(3, 1)
    take_w(4, 2)
    take_w(4, 3)
    build(4)
    each(XN, lambda d: cp_px(d).wait_recv(), 0)
    for t in range(1, 6):
        for direction in range(2):
            cp_pz(direction, t).wait_recv()
    cp_pz(0, 6).wait_recv()
    take_w(4, 0)
    take_w(4, 1)
    sum_x()
    multiply(slice(0, 512), wy[:, :, :, 0:512].reshape(ALLH, 512))
    multiply(slice(512, PLAIN), wy[:, :, :, 512:PLAIN].reshape(ALLH, PLAIN - 512))
    shares(range(7))
    for p in range(XN):
        low = PLAIN + p * SHARE
        multiply(slice(low, low + SHARE), wsh[p].reshape(ALLH, SHARE))

    table = None
    for r in range(REL):
        out = jnp.dot(c_ref[r], m_ref[:, r * HALF:(r + 1) * HALF], preferred_element_type=f32)
        table = out if table is None else table + out
    for p in range(YN):
        tsend[p] = table[p * 64:(p + 1) * 64].astype(bf16)
    for h in range(2):
        start(lambda d, h=h: cp_t(d, h), YN)

    arrive(cp_wz, ZN)
    total = wz[z].astype(f32)
    for d in range(1, ZN):
        total = total + wbz[(z + ZN - d) % ZN].astype(f32)
    gz[z] = total.astype(bf16)
    start(cp_gz, ZN)

    for h in range(2):
        arrive(lambda d: cp_t(d, h), YN)
        rows = slice(32 * h, 32 * h + 32)
        total = tsend[y, rows].astype(f32)
        for d in range(1, YN):
            total = total + tbuf[(y + YN - d) % YN, rows].astype(f32)
        tall[core, y, rows] = total.astype(bf16)
        start(lambda d, h=h: cp_ta(d, h), YN)
        start1(cp_tc(0, h))
    arrive(cp_gz, ZN)
    start(cp_gx, XN)

    for h in range(2):
        def hand_on(d):
            cp_ta(d, h).wait_recv()
            cp_tc(d, h).start()

        each(YN, hand_on)
        pending.append((lambda d, h=h: cp_tc(d, h), YN))
    arrive(cp_gx, XN)
    gx[x] = gz[...]
    for p in range(XN):
        for k in range(ZN):
            gout[p * 16:(p + 1) * 16, window_start(k):window_start(k) + GWIN] = gx[p, k]

    for h in range(2):
        each(YN, lambda d: cp_tc(d, h, other).wait_recv(), 0)
    for c in range(2):
        for p in range(YN):
            tout[p * 64:(p + 1) * 64, c * HALF:(c + 1) * HALF] = tall[c, p]

    for fn, n in pending:
        each(n, lambda d: fn(d).wait_send())


def body(agg_rows, seed_feats, seed_type, w_rel, w_self, cotangent, counts, owner, local_row):
    y = lax.axis_index("narrow") // 2
    count = lax.dynamic_slice_in_dim(counts, y * GROUP, GROUP, 0)
    slots = GROUP * REL * FAN
    names = lax.dynamic_slice_in_dim(owner[:, 0] * NODES_DEV + local_row, y * slots, slots, 0)
    live = lax.broadcasted_iota(i32, (1, 1, FAN), 2) < count[:, :, None]
    key = jnp.where(live.reshape(GROUP, REL * FAN), names.reshape(GROUP, REL * FAN), DEAD)
    key = key[:8] + key[8:] * 65536
    vmem = pltpu.VMEM
    dma = lambda n: pltpu.SemaphoreType.DMA((n,))
    pairs = lambda *sizes: [dma(n) for n in sizes for _ in range(2)]
    table, grads = pl.pallas_call(
        kernel,
        out_shape=(jax.ShapeDtypeStruct((NODES_DEV, F), bf16), jax.ShapeDtypeStruct((HID, GCOLS), bf16)),
        in_specs=[pl.BlockSpec(memory_space=vmem)] * 7,
        out_specs=(pl.BlockSpec(memory_space=vmem),) * 2,
        scratch_shapes=[
            vmem((2, HID, REL * HALF), bf16),
            vmem((2, YN, HID, PLAIN), bf16),
            vmem((XN, 2, YN, HID, SHARE), bf16),
            vmem((YN, GROUP, 128), bf16),
            vmem((YN, GROUP, 128), bf16),
            vmem((ZN, XN, GROUP, ALLH), bf16),
            vmem((ROWS, REL * HALF), bf16),
            vmem((REL, ROWS, 128), f32),
            vmem((ZN, XN, 8, 128), i32),
            vmem((2, 128, ROWS), f32),
            vmem((REL, NODES_DEV, ROWS), bf16),
            vmem((XN, 16, GCOLS), bf16),
            vmem((XN, 16, GCOLS), bf16),
            vmem((ZN, 16, GWIN), bf16),
            vmem((ZN, 16, GWIN), bf16),
            vmem((ZN, 16, GWIN), bf16),
            vmem((XN, ZN, 16, GWIN), bf16),
            vmem((YN, 64, HALF), bf16),
            vmem((YN, 64, HALF), bf16),
            vmem((2, YN, 64, HALF), bf16),
            *pairs(REL, XN, ZN, ZN, YN, XN, ZN, 32, 28, XN, XN, 8, 24, 12, ZN, XN, 16, 16, 16),
        ],
        compiler_params=pltpu.CompilerParams(
            collective_id=0, has_side_effects=True, vmem_limit_bytes=56 * 1024 * 1024),
        cost_estimate=pl.CostEstimate(flops=6_500_000_000, bytes_accessed=8_000_000, transcendentals=8192),
    )(agg_rows, w_rel.T, seed_feats, w_self.transpose(0, 2, 1), seed_type.reshape(1, -1), cotangent.T, key)
    grad_rel = grads[:, :REL * F].astype(f32).T
    grad_self = jnp.stack([grads[:, (REL + t) * F:(REL + t + 1) * F].astype(f32).T for t in range(2)])
    return table.astype(f32), grad_rel, grad_self


def solution(mesh):
    in_specs = (
        P("wide", None),
        P("wide", None),
        P("wide"),
        P(None, "narrow"),
        P(None, None, "narrow"),
        P("wide", "narrow"),
        P("wide", None),
        P("wide", None),
        P("wide"),
    )
    out_specs = (P("wide", None), P(None, "narrow"), P(None, None, "narrow"))
    return jax.shard_map(body, mesh=mesh, in_specs=in_specs, out_specs=out_specs, check_vma=False)
```
